32 devices in a mesh: gy: 8 (over z, core), gx: 4 (over y, x).
Axes of the slice: x: 2, y: 2, z: 4, core: 2. Of those that a mesh axis runs over, the one named last changes fastest.
Arguments:
- incoming_activations: bfloat16 [192, 64, 1024], P(None, 'gy', 'gx'), may hold values from -75 to 75
- upstream_adjoint: bfloat16 [192, 64, 1024], P(None, 'gy', 'gx'), may hold values from -30 to 30
- standardize_factor: float32 [192], replicated, may hold values from 0.1 to 1.9
- standardize_offset: float32 [192], replicated, may hold values from -3 to 3
- triple_mapping_matrix: bfloat16 [576, 192], replicated, may hold values from -0.4375 to 0.4375
- spatial_filter_taps: float32 [3, 3, 576], replicated, may hold values from -2 to 2
- sharpness_factor: float32 [4], replicated, may hold values from 1 to 8
- output_mapping_matrix: bfloat16 [192, 192], replicated, may hold values from -0.4375 to 0.4375
Outputs:
- incoming_activation_adjoint: bfloat16 [192, 64, 1024], P(None, 'gy', 'gx')
- triple_mapping_adjoint: float32 [576, 192], replicated
- spatial_filter_adjoint: float32 [3, 3, 576], replicated
- output_mapping_adjoint: float32 [192, 192], replicated
- sharpness_factor_adjoint: float32 [4], replicated
- standardize_factor_adjoint: float32 [192], replicated
- standardize_offset_adjoint: float32 [192], replicated
The draws below stay inside these ranges and needn't reach their ends.
All inputs are finite; a program needn't handle non-finite values.
Results may differ from the reference program's by a relative error of at most 0.0063.
Values may be sent and summed in bfloat16 or wider, within the bound.
A program may use at most 128 MiB of HBM per device.

```python
import math
import jax
import jax.numpy as jnp
from jax import lax

ATTENDER_TOTAL = 4
HD = 48
C = 192
QKV = 576
NY = 64
NX = 1024
TEXELS = 65536


def draw_incoming_activations(key, part):
    key = jax.random.fold_in(key, 11)
    noise_key, scale_key = jax.random.split(key)
    noise = jnp.clip(jax.random.normal(noise_key, (C, NY, NX), jnp.float32), -6.0, 6.0)
    scales = jnp.exp(jax.random.uniform(scale_key, (C, 1, 1), jnp.float32, 0.0, math.log(10.0)))
    return (scales * noise).astype(jnp.bfloat16)


def draw_upstream_adjoint(key, part):
    key = jax.random.fold_in(key, 23)
    mean_key, noise_key = jax.random.split(key, 2)
    means = jnp.clip(0.5 * jax.random.normal(mean_key, (C, 1, 1), jnp.float32), -2.0, 2.0)
    row_pos = jnp.arange(NY, dtype=jnp.float32)[:, None] / (NY - 1)
    col_pos = jnp.arange(NX, dtype=jnp.float32)[None, :] / (NX - 1)
    ramp = 1.0 + row_pos + col_pos
    noise = jnp.clip(jax.random.normal(noise_key, (C, NY, NX), jnp.float32), -6.0, 6.0)
    return ((means + noise) * ramp[None]).astype(jnp.bfloat16)


def scatter_about(own_key, shape, width, limit, held_as=jnp.bfloat16):
    drawn = jax.random.normal(own_key, shape, jnp.float32) * width
    return jnp.minimum(jnp.maximum(drawn, -limit), limit).astype(held_as)


def setup_inputs(seed: int = 0) -> dict:
    key_of = jax.random.split(jax.random.key(seed), 9)
    return {
        "incoming_activations": draw_incoming_activations(jax.random.fold_in(key_of[8], 71), 0),
        "upstream_adjoint": draw_upstream_adjoint(jax.random.fold_in(key_of[8], 71), 0),
        "standardize_factor": jnp.clip(1.0 + 0.18 * jax.random.normal(key_of[2], (C,), jnp.float32), 0.1, 1.9),
        "standardize_offset": scatter_about(key_of[3], (C,), 0.5, 3.0, jnp.float32),
        "triple_mapping_matrix": scatter_about(key_of[4], (QKV, C), C ** -0.5, 0.4375),
        "spatial_filter_taps": scatter_about(key_of[5], (3, 3, QKV), 9 ** -0.5, 2.0, jnp.float32),
        "sharpness_factor": jnp.clip(jnp.exp(jax.random.uniform(key_of[6], (ATTENDER_TOTAL,), jnp.float32, math.log(1.0), math.log(8.0))), 1.0, 8.0),
        "output_mapping_matrix": scatter_about(key_of[7], (C, C), C ** -0.5, 0.4375),
    }


def grouped_conv(field, tap_weights):
    groups = field.reshape(-1, HD, NY, NX)
    group_taps = jnp.moveaxis(tap_weights.reshape(3, 3, -1, HD), 2, 0)

    def one_group(pair):
        piece, piece_taps = pair
        padded = jnp.pad(piece, ((0, 0), (1, 1), (1, 1)))
        summed = jnp.zeros(piece.shape, jnp.float32)
        for row_off in range(3):
            for col_off in range(3):
                window = padded[:, row_off:row_off + NY, col_off:col_off + NX].astype(jnp.float32)
                summed = summed + piece_taps[row_off, col_off][:, None, None] * window
        return summed.astype(jnp.bfloat16)
    return lax.map(one_group, (groups, group_taps)).reshape(field.shape)

def tap_sums(grad_field, field):
    grad_groups = grad_field.reshape(-1, HD, NY, NX)
    groups = field.reshape(-1, HD, NY, NX)

    def one_group(pair):
        grad_piece, piece = pair
        grad_f32 = grad_piece.astype(jnp.float32)
        padded = jnp.pad(piece, ((0, 0), (1, 1), (1, 1)))
        rows_out = []
        for row_off in range(3):
            line = []
            for col_off in range(3):
                window = padded[:, row_off:row_off + NY, col_off:col_off + NX].astype(jnp.float32)
                line.append(lax.optimization_barrier(jnp.sum(grad_f32 * window, axis=(1, 2))))
            rows_out.append(jnp.stack(line))
        return jnp.stack(rows_out)
    per_group = lax.map(one_group, (grad_groups, groups))
    return jnp.moveaxis(per_group, 0, 2).reshape(3, 3, -1)

def reference(incoming_activations, upstream_adjoint, standardize_factor, standardize_offset, triple_mapping_matrix, spatial_filter_taps, sharpness_factor, output_mapping_matrix):
    f32 = jnp.float32
    half_precision_type = jnp.bfloat16
    pixel_total = float(TEXELS)
    x_flat = incoming_activations.astype(f32).reshape(C, TEXELS)
    average = lax.optimization_barrier(jnp.mean(x_flat, axis=0, keepdims=True))
    centred = x_flat - average
    inv_std = 1.0 / jnp.sqrt(lax.optimization_barrier(jnp.mean(centred * centred, axis=0, keepdims=True)) + 1e-05)
    x_hat = centred * inv_std
    normed = (x_hat * standardize_factor[:, None] + standardize_offset[:, None]).astype(half_precision_type)

    def project_block(weight_rows):
        return jnp.dot(weight_rows, normed, preferred_element_type=f32).astype(half_precision_type)
    projected = lax.map(project_block, triple_mapping_matrix.reshape(3 * ATTENDER_TOTAL, HD, C)).reshape(QKV, NY, NX)
    conv_out = grouped_conv(projected, spatial_filter_taps).reshape(3, ATTENDER_TOTAL, HD, TEXELS)
    queries, key_rows, value_rows = (conv_out[0], conv_out[1], conv_out[2])
    q_f32 = queries.astype(f32)
    k_f32 = key_rows.astype(f32)
    v_f32 = value_rows.astype(f32)
    squares_q = lax.optimization_barrier(jnp.sum(q_f32 * q_f32, axis=2))
    squares_k = lax.optimization_barrier(jnp.sum(k_f32 * k_f32, axis=2))
    similarity_matrix = jnp.einsum('hin,hjn->hij', q_f32, k_f32)
    unit_probe_vectors = jnp.sqrt(squares_q + 1e-06)
    unit_lookup_vectors = jnp.sqrt(squares_k + 1e-06)
    affinity_matrix = sharpness_factor[:, None, None] * similarity_matrix / (unit_probe_vectors[:, :, None] * unit_lookup_vectors[:, None, :])
    expo = jnp.exp(affinity_matrix)
    attend = expo / lax.optimization_barrier(jnp.sum(expo, axis=2, keepdims=True))
    attend_low = attend.astype(half_precision_type)
    attended = jnp.einsum('hij,hjn->hin', attend_low.astype(f32), v_f32).astype(half_precision_type).reshape(C, TEXELS)
    grad_flat = upstream_adjoint.reshape(C, TEXELS)
    output_mapping_adjoint = jnp.dot(grad_flat, attended.T, preferred_element_type=f32) / pixel_total
    grad_attended = jnp.dot(output_mapping_matrix.T, grad_flat, preferred_element_type=f32).astype(half_precision_type).reshape(ATTENDER_TOTAL, HD, TEXELS)
    ga_f32 = grad_attended.astype(f32)
    grad_attend = jnp.einsum('hin,hjn->hij', ga_f32, v_f32)
    grad_values = jnp.einsum('hij,hin->hjn', attend_low.astype(f32), ga_f32)
    affinity_matrix_adjoint = attend * (grad_attend - lax.optimization_barrier(jnp.sum(attend * grad_attend, axis=2, keepdims=True)))
    mixed_content_vectors = affinity_matrix_adjoint * affinity_matrix
    sharpness_factor_adjoint = lax.optimization_barrier(jnp.sum(mixed_content_vectors, axis=(1, 2))) / sharpness_factor / pixel_total
    row_terms = lax.optimization_barrier(jnp.sum(mixed_content_vectors, axis=2))
    col_terms = lax.optimization_barrier(jnp.sum(mixed_content_vectors, axis=1))
    plane_mixing_matrix = (sharpness_factor[:, None, None] * affinity_matrix_adjoint / (unit_probe_vectors[:, :, None] * unit_lookup_vectors[:, None, :])).astype(half_precision_type)
    cp_f32 = plane_mixing_matrix.astype(f32)
    grad_queries = jnp.einsum('hij,hjn->hin', cp_f32, k_f32) - (row_terms / (squares_q + 1e-06))[:, :, None] * q_f32
    grad_keys = jnp.einsum('hij,hin->hjn', cp_f32, q_f32) - (col_terms / (squares_k + 1e-06))[:, :, None] * k_f32
    grad_conv = jnp.stack([grad_queries, grad_keys, grad_values]).astype(half_precision_type).reshape(QKV, NY, NX)
    grad_projected = grouped_conv(grad_conv, spatial_filter_taps[::-1, ::-1]).reshape(QKV, TEXELS)
    spatial_filter_adjoint = tap_sums(grad_conv, projected) / pixel_total
    triple_mapping_adjoint = jnp.dot(grad_projected, normed.T, preferred_element_type=f32) / pixel_total
    grad_normed = jnp.dot(triple_mapping_matrix.T, grad_projected, preferred_element_type=f32)
    standardize_factor_adjoint = lax.optimization_barrier(jnp.sum(grad_normed * x_hat, axis=1)) / pixel_total
    standardize_offset_adjoint = lax.optimization_barrier(jnp.sum(grad_normed, axis=1)) / pixel_total
    grad_hat = grad_normed * standardize_factor[:, None]
    centre_term = lax.optimization_barrier(jnp.mean(grad_hat, axis=0, keepdims=True))
    slope_term = lax.optimization_barrier(jnp.mean(grad_hat * x_hat, axis=0, keepdims=True))
    incoming_activation_adjoint = grad_flat.astype(f32) + inv_std * (grad_hat - centre_term - x_hat * slope_term)
    incoming_activation_adjoint = incoming_activation_adjoint.astype(half_precision_type).reshape(C, NY, NX)
    return (incoming_activation_adjoint, triple_mapping_adjoint, spatial_filter_adjoint, output_mapping_adjoint, sharpness_factor_adjoint, standardize_factor_adjoint, standardize_offset_adjoint)
```

```python
import functools

import jax
import jax.numpy as jnp
import numpy as np
from jax import lax
from jax.experimental import pallas as pl
from jax.experimental.pallas import tpu as pltpu
from jax.sharding import PartitionSpec as P

ATTENDER_TOTAL = 4
HD = 48
F32 = jnp.float32
BF16 = jnp.bfloat16
MESH = pl.DeviceIdType.MESH
VMEM = pl.BlockSpec(memory_space=pltpu.VMEM)
SMEM = pl.BlockSpec(memory_space=pltpu.SMEM)
NT = (((1,), (1,)), ((), ()))
TN = (((0,), (0,)), ((), ()))
LIMIT = 56 * 1024 * 1024
SIDE = 16


def dot(a, b, dims=(((1,), (0,)), ((), ()))):
    return lax.dot_general(a, b, dims, preferred_element_type=F32)


def dot_full(a, b, dims=(((1,), (0,)), ((), ()))):
    return lax.dot_general(
        a, b, dims, preferred_element_type=F32, precision=lax.Precision.HIGHEST
    )


def front_kernel(rows, cols, x_ref, gain_ref, bias_ref, w_ref, sel_ref,
                 p_ref, normed_ref, stat_ref, edge_ref):
    channels = x_ref.shape[0]
    gain = gain_ref[...]
    bias = bias_ref[...]
    edge = jnp.zeros((2 * SIDE, channels), F32)
    normed_ref[pl.ds(channels, normed_ref.shape[0] - channels), :] = jnp.zeros(
        (normed_ref.shape[0] - channels, rows * cols), BF16
    )
    stat_ref[...] = jnp.zeros_like(stat_ref)
    for y in range(rows):
        at = pl.ds(y * cols, cols)
        x = x_ref[:, at].astype(F32)
        mean = jnp.sum(x, axis=0, keepdims=True) / channels
        centred = x - mean
        var = jnp.sum(centred * centred, axis=0, keepdims=True) / channels
        inv = 1.0 / jnp.sqrt(var + 1e-05)
        stat_ref[pl.ds(0, 1), at] = mean
        stat_ref[pl.ds(1, 1), at] = inv
        normed = ((centred * inv) * gain + bias).astype(BF16)
        normed_ref[pl.ds(0, channels), at] = normed
        p_ref[:, at] = dot(w_ref[...], normed).astype(BF16)
        edge = edge + dot(sel_ref[:, at], normed, NT)
    edge_ref[...] = dot(edge.astype(BF16), w_ref[...], NT).astype(BF16)


def halo_kernel(cols, p_ref, edge_ref, top_ref, bot_ref, side_ref, send, recv):
    gy, gx = lax.axis_index("gy"), lax.axis_index("gx")
    ny, nx = lax.axis_size("gy"), lax.axis_size("gx")
    tail = p_ref.shape[1] - cols
    moves = []
    for dy in (-1, 0, 1):
        for dx in (-1, 0, 1):
            if dy or dx:
                moves.append((dy, dx))

    def there(dy, dx):
        ty, tx = gy + dy, gx + dx
        return (ty >= 0) & (ty < ny) & (tx >= 0) & (tx < nx), (ty, tx)

    barrier = pltpu.get_barrier_semaphore()
    for dy, dx in moves:
        ok, target = there(dy, dx)

        @pl.when(ok)
        def _(target=target):
            pl.semaphore_signal(barrier, inc=1, device_id=target, device_id_type=MESH)

    down = 1 + (gy > 0).astype(jnp.int32) + (gy < ny - 1).astype(jnp.int32)
    across = 1 + (gx > 0).astype(jnp.int32) + (gx < nx - 1).astype(jnp.int32)
    pl.semaphore_wait(barrier, down * across - 1)

    def copy(k, dy, dx, target):
        if dx == 0:
            src = p_ref.at[:, pl.ds(0 if dy < 0 else tail, cols)]
            dst = bot_ref if dy < 0 else top_ref
        else:
            src = edge_ref.at[pl.ds(0 if dx < 0 else SIDE, SIDE)]
            dst = side_ref.at[1 if dx < 0 else 0, 1 - dy]
        return pltpu.make_async_remote_copy(
            src_ref=src, dst_ref=dst, send_sem=send.at[k], recv_sem=recv.at[k],
            device_id=target, device_id_type=MESH,
        )

    for k, (dy, dx) in enumerate(moves):
        ok, target = there(dy, dx)

        @pl.when(ok)
        def _(k=k, dy=dy, dx=dx, target=target):
            copy(k, dy, dx, target).start()

    for k, (dy, dx) in enumerate(moves):
        ok, target = there(-dy, -dx)
        back, other = there(dy, dx)

        @pl.when(ok)
        def _(k=k, dy=dy, dx=dx, target=target):
            copy(k, dy, dx, target).wait_recv()

        @pl.when(jnp.logical_not(ok))
        def _(k=k, dy=dy, dx=dx):
            if dx == 0:
                ref = bot_ref if dy < 0 else top_ref
                ref[...] = jnp.zeros_like(ref)
            else:
                side_ref[1 if dx < 0 else 0, 1 - dy] = jnp.zeros(side_ref.shape[2:], BF16)

        @pl.when(back)
        def _(k=k, dy=dy, dx=dx, other=other):
            copy(k, dy, dx, other).wait_send()


def halo(p, edge, cols, collective_id):
    width = p.shape[0]
    return pl.pallas_call(
        functools.partial(halo_kernel, cols),
        out_shape=(
            jax.ShapeDtypeStruct((width, cols), BF16),
            jax.ShapeDtypeStruct((width, cols), BF16),
            jax.ShapeDtypeStruct((2, 3, SIDE, width), BF16),
        ),
        in_specs=[VMEM] * 2,
        out_specs=(VMEM,) * 3,
        scratch_shapes=[pltpu.SemaphoreType.DMA((8,)), pltpu.SemaphoreType.DMA((8,))],
        compiler_params=pltpu.CompilerParams(
            collective_id=collective_id, has_side_effects=True, vmem_limit_bytes=LIMIT
        ),
    )(p, edge)


def shift_rows(rows, cols, p_ref, top_ref, bot_ref, side_ref, shift_ref, spread_ref, moved):
    width = p_ref.shape[0]
    for y in range(rows + 2):
        at = pl.ds(y * cols, cols)
        if y == 0:
            row = top_ref[...]
        elif y == rows + 1:
            row = bot_ref[...]
        else:
            row = p_ref[:, pl.ds((y - 1) * cols, cols)]
        for side in range(2):
            edge = side_ref[side].reshape(3 * SIDE, width)
            fill = dot(edge, spread_ref[side, :, at], TN)
            moved[side, :, at] = (dot(row, shift_ref[side]) + fill).astype(BF16)


def conv_kernel(rows, cols, p_ref, top_ref, bot_ref, side_ref, shift_ref, spread_ref, taps_ref,
                g_ref, conv_ref, part_ref, moved, squares):
    width = p_ref.shape[0]
    channels = width // 3
    part_rows = part_ref.shape[0]
    shift_rows(rows, cols, p_ref, top_ref, bot_ref, side_ref, shift_ref, spread_ref, moved)

    def chunk(i, carry):
        rs = pl.ds(pl.multiple_of(i * 16, 16), 16)
        taps = [jnp.broadcast_to(taps_ref[rs, pl.ds(k, 1)], (16, 128)) for k in range(9)]
        total = jnp.zeros((16, 128), F32)
        for half in range(cols // 128):
            got = {}
            for y in range(rows + 2):
                at = pl.ds(y * cols + half * 128, 128)
                if y == 0:
                    mid = top_ref[rs, pl.ds(half * 128, 128)]
                elif y == rows + 1:
                    mid = bot_ref[rs, pl.ds(half * 128, 128)]
                else:
                    mid = p_ref[rs, pl.ds((y - 1) * cols + half * 128, 128)]
                got[y] = (moved[0, rs, at].astype(F32), mid.astype(F32), moved[1, rs, at].astype(F32))
                if y >= 2:
                    out = jnp.zeros((16, 128), F32)
                    for a in range(3):
                        for b in range(3):
                            out = out + taps[3 * a + b] * got[y - 2 + a][b]
                    out = out.astype(BF16)
                    conv_ref[rs, pl.ds((y - 2) * cols + half * 128, 128)] = out
                    out = out.astype(F32)
                    total = total + out * out
        squares[rs, :] = jnp.broadcast_to(jnp.sum(total, axis=1, keepdims=True), (16, 128))
        return carry

    lax.fori_loop(0, width // 16, chunk, 0)
    queries = conv_ref[pl.ds(0, channels), :]
    keys = conv_ref[pl.ds(channels, channels), :]
    values = conv_ref[pl.ds(2 * channels, channels), :]
    gram = dot(queries, keys, NT)
    mixed = dot(g_ref[...], values, NT)
    lane = lax.broadcasted_iota(jnp.int32, (HD, channels), 1) // HD
    compact = jnp.zeros((HD, channels), F32)
    for h in range(channels // HD):
        compact = compact + jnp.where(lane == h, gram[h * HD:(h + 1) * HD, :], 0.0)
    pad = jnp.zeros((channels, 256 - channels), F32)
    lanes = lax.broadcasted_iota(jnp.int32, (channels, 128), 1)
    high = jnp.concatenate([mixed[:, 128:], pad], axis=1)
    high = jnp.where(lanes == 64, squares[pl.ds(0, channels), :], high)
    high = jnp.where(lanes == 65, squares[pl.ds(channels, channels), :], high)
    span = channels + HD
    part_ref[pl.ds(0, channels), :] = mixed[:, :128]
    part_ref[pl.ds(channels, HD), :] = compact[:, :128]
    part_ref[pl.ds(span, channels), :] = high
    part_ref[pl.ds(span + channels, HD), :] = jnp.concatenate(
        [compact[:, 128:], pad[:HD]], axis=1
    )
    part_ref[pl.ds(2 * span, part_rows - 2 * span), :] = jnp.zeros((part_rows - 2 * span, 128), F32)


def sum_kernel(in_ref, out_ref, got_x, held, got_y, send, recv):
    gy, gx = lax.axis_index("gy"), lax.axis_index("gx")
    ny, nx = lax.axis_size("gy"), lax.axis_size("gx")
    barrier = pltpu.get_barrier_semaphore()
    for d in range(1, nx):
        pl.semaphore_signal(barrier, inc=1, device_id=(gy, lax.rem(gx + d, nx)), device_id_type=MESH)
    for d in range(1, ny):
        pl.semaphore_signal(barrier, inc=1, device_id=(lax.rem(gy + d, ny), gx), device_id_type=MESH)
    pl.semaphore_wait(barrier, nx + ny - 2)

    slot = 0

    def exchange(copies):
        nonlocal slot
        made = []
        for src, dst, target in copies:
            made.append(pltpu.make_async_remote_copy(
                src_ref=src, dst_ref=dst, send_sem=send.at[slot], recv_sem=recv.at[slot],
                device_id=target, device_id_type=MESH,
            ))
            slot += 1
            made[-1].start()
        for copy in made:
            copy.wait()

    exchange([
        (in_ref.at[lax.rem(gx + d, nx)], got_x.at[d - 1], (gy, lax.rem(gx + d, nx)))
        for d in range(1, nx)
    ])
    total = in_ref[gx]
    for d in range(1, nx):
        total = total + got_x[d - 1]
    held[...] = total
    exchange([
        (held.at[lax.rem(gy + d, ny)], got_y.at[d - 1], (lax.rem(gy + d, ny), gx))
        for d in range(1, ny)
    ])
    total = held[gy]
    for d in range(1, ny):
        total = total + got_y[d - 1]
    out_ref[gx, gy] = total
    exchange([
        (out_ref.at[gx, gy], out_ref.at[gx, gy], (lax.rem(gy + d, ny), gx)) for d in range(1, ny)
    ])
    exchange([
        (out_ref.at[gx], out_ref.at[gx], (gy, lax.rem(gx + d, nx))) for d in range(1, nx)
    ])


def sum_over_devices(part, collective_id):
    ny, nx = lax.axis_size("gy"), lax.axis_size("gx")
    piece = part.shape[0] // (nx * ny)
    count = 2 * (nx + ny - 2)
    shape = (nx, ny, piece, 128)
    out = pl.pallas_call(
        sum_kernel,
        out_shape=jax.ShapeDtypeStruct(shape, F32),
        in_specs=[VMEM],
        out_specs=VMEM,
        scratch_shapes=[
            pltpu.VMEM((nx - 1, ny, piece, 128), F32),
            pltpu.VMEM((ny, piece, 128), F32),
            pltpu.VMEM((ny - 1, piece, 128), F32),
            pltpu.SemaphoreType.DMA((count,)),
            pltpu.SemaphoreType.DMA((count,)),
        ],
        compiler_params=pltpu.CompilerParams(
            collective_id=collective_id, has_side_effects=True, vmem_limit_bytes=LIMIT
        ),
    )(part.reshape(shape))
    return out.reshape(part.shape)


def padded_rows(count):
    unit = 8 * lax.axis_size("gy") * lax.axis_size("gx")
    return -(-count // unit) * unit


def attend_kernel(texels, tot_ref, sharp_ref, wo_ref, conv_ref, g_ref, sel_ref,
                  grad_ref, edge_ref, omap_ref, sharp_adj_ref):
    channels = wo_ref.shape[0]
    span = channels + HD
    low, high = tot_ref[pl.ds(0, channels), :], tot_ref[pl.ds(span, channels), :]
    mixed = jnp.concatenate([low, high[:, :channels - 128]], axis=1)
    sq, sk = high[:, 64:65], high[:, 65:66]
    compact = jnp.concatenate(
        [tot_ref[pl.ds(channels, HD), :], tot_ref[pl.ds(span + channels, HD), :][:, :channels - 128]],
        axis=1,
    )
    heads = channels // HD
    gram = jnp.concatenate([compact] * heads, axis=0)
    rows = lax.broadcasted_iota(jnp.int32, (channels, channels), 0)
    lanes = lax.broadcasted_iota(jnp.int32, (channels, channels), 1)
    same = (rows // HD) == (lanes // HD)
    eye = rows == lanes
    head = lax.broadcasted_iota(jnp.int32, (channels, 1), 0) // HD
    sharp = jnp.zeros((channels, 1), F32)
    for h in range(heads):
        sharp = jnp.where(head == h, sharp_ref[h], sharp)

    def to_row(col):
        return jnp.sum(jnp.where(eye, col, 0.0), axis=0, keepdims=True)

    def to_col(row):
        return jnp.sum(jnp.where(eye, row, 0.0), axis=1, keepdims=True)

    norms = jnp.sqrt(sq + 1e-06) * jnp.sqrt(to_row(sk) + 1e-06)
    logits = jnp.where(same, sharp * gram / norms, 0.0)
    expo = jnp.where(same, jnp.exp(logits), 0.0)
    attend = expo / jnp.sum(expo, axis=1, keepdims=True)
    attend_low = attend.astype(BF16)
    omap_ref[...] = dot_full(mixed, attend_low.astype(F32), NT) / texels
    grad_attend = dot_full(wo_ref[...].astype(F32), mixed, TN)
    grad_logits = attend * (grad_attend - jnp.sum(attend * grad_attend, axis=1, keepdims=True))
    product = grad_logits * logits
    row_terms = jnp.sum(product, axis=1, keepdims=True)
    col_terms = to_col(jnp.sum(product, axis=0, keepdims=True))
    for h in range(heads):
        sharp_adj_ref[h] = jnp.sum(jnp.where(head == h, row_terms, 0.0)) / sharp_ref[h] / texels
    coupling = (sharp * grad_logits / norms).astype(BF16)
    row_scale = row_terms / (sq + 1e-06)
    col_scale = col_terms / (sk + 1e-06)
    cells = conv_ref.shape[1]
    step = 256
    edges = [jnp.zeros((2 * SIDE, channels), F32) for _ in range(3)]
    for n in range(cells // step):
        at = pl.ds(n * step, step)
        queries = conv_ref[pl.ds(0, channels), at]
        keys = conv_ref[pl.ds(channels, channels), at]
        grad_attended = dot(wo_ref[...], g_ref[:, at], TN).astype(BF16)
        grads = (
            dot(coupling, keys) - row_scale * queries.astype(F32),
            dot(coupling, queries, TN) - col_scale * keys.astype(F32),
            dot(attend_low, grad_attended, TN),
        )
        for i, grad in enumerate(grads):
            grad = grad.astype(BF16)
            grad_ref[pl.ds(i * channels, channels), at] = grad
            edges[i] = edges[i] + dot(sel_ref[:, at], grad, NT)
    edge_ref[...] = jnp.concatenate(edges, axis=1).astype(BF16)


def back_kernel(rows, cols, texels, grad_ref, top_ref, bot_ref, side_ref, shift_ref, spread_ref,
                taps_ref, p_ref, normed_ref, w_ref, x_ref, stat_ref, gain_ref, g_ref,
                out_ref, part_ref, moved, gp_ref, sums):
    width = grad_ref.shape[0]
    channels = width // 3
    part_rows = part_ref.shape[0]
    shift_rows(rows, cols, grad_ref, top_ref, bot_ref, side_ref, shift_ref, spread_ref, moved)

    def chunk(i, carry):
        rs = pl.ds(pl.multiple_of(i * 16, 16), 16)
        taps = [jnp.broadcast_to(taps_ref[rs, pl.ds(k, 1)], (16, 128)) for k in range(9)]
        tap_sums = [jnp.zeros((16, 128), F32) for _ in range(9)]
        for half in range(cols // 128):
            got = {}
            for y in range(rows + 2):
                at = pl.ds(y * cols + half * 128, 128)
                if y == 0:
                    mid = top_ref[rs, pl.ds(half * 128, 128)]
                elif y == rows + 1:
                    mid = bot_ref[rs, pl.ds(half * 128, 128)]
                else:
                    mid = grad_ref[rs, pl.ds((y - 1) * cols + half * 128, 128)]
                got[y] = (moved[0, rs, at].astype(F32), mid.astype(F32), moved[1, rs, at].astype(F32))
                if y >= 2:
                    here = pl.ds((y - 2) * cols + half * 128, 128)
                    field = p_ref[rs, here].astype(F32)
                    out = jnp.zeros((16, 128), F32)
                    for a in range(3):
                        for b in range(3):
                            k = 3 * (2 - a) + (2 - b)
                            out = out + taps[k] * got[y - 2 + a][b]
                            tap_sums[k] = tap_sums[k] + field * got[y - 2 + a][b]
                    gp_ref[rs, here] = out.astype(BF16)
        lane = lax.broadcasted_iota(jnp.int32, (16, 128), 1)
        packed = jnp.zeros((16, 128), F32)
        for k in range(9):
            packed = jnp.where(lane == 64 + k, jnp.sum(tap_sums[k], axis=1, keepdims=True), packed)
        sums[rs, :] = packed
        return carry

    lax.fori_loop(0, width // 16, chunk, 0)
    gain = gain_ref[...]
    gain_sum = jnp.zeros((channels, cols), F32)
    bias_sum = jnp.zeros((channels, cols), F32)
    for y in range(rows):
        at = pl.ds(y * cols, cols)
        grad_normed = dot(w_ref[...], gp_ref[:, at], TN)
        mean, inv = stat_ref[pl.ds(0, 1), at], stat_ref[pl.ds(1, 1), at]
        x_hat = (x_ref[:, at].astype(F32) - mean) * inv
        gain_sum = gain_sum + grad_normed * x_hat
        bias_sum = bias_sum + grad_normed
        grad_hat = grad_normed * gain
        centre = jnp.sum(grad_hat, axis=0, keepdims=True) / channels
        slope = jnp.sum(grad_hat * x_hat, axis=0, keepdims=True) / channels
        out = g_ref[:, at].astype(F32) + inv * (grad_hat - centre - x_hat * slope)
        out_ref[:, at] = out.astype(BF16)
    lane = lax.broadcasted_iota(jnp.int32, (channels, 128), 1)
    first = sums[pl.ds(0, channels), :]
    first = jnp.where(lane == 73, jnp.sum(gain_sum, axis=1, keepdims=True), first)
    first = jnp.where(lane == 74, jnp.sum(bias_sum, axis=1, keepdims=True), first)
    sums[pl.ds(0, channels), :] = first
    for i in range(3):
        rs = pl.ds(i * channels, channels)
        weight = dot(gp_ref[rs, :], normed_ref[...], NT)
        part_ref[rs, :] = weight[:, :128] / texels
        part_ref[pl.ds(width + i * channels, channels), :] = (weight[:, 128:] + sums[rs, :]) / texels
    part_ref[pl.ds(2 * width, part_rows - 2 * width), :] = jnp.zeros((part_rows - 2 * width, 128), F32)


def call(kernel, out_shape, args, in_specs=None, out_specs=None, scratch=()):
    return pl.pallas_call(
        kernel,
        out_shape=out_shape,
        in_specs=in_specs or [VMEM] * len(args),
        out_specs=out_specs or (VMEM,) * len(out_shape),
        scratch_shapes=scratch,
        compiler_params=pltpu.CompilerParams(vmem_limit_bytes=LIMIT),
    )(*args)


def constants(rows, cols):
    cells, wide = rows * cols, (rows + 2) * cols
    pick = np.zeros((2 * SIDE, cells), np.float32)
    shift = np.zeros((2, cols, cols), np.float32)
    spread = np.zeros((2, 3, SIDE, wide), np.float32)
    for y in range(rows):
        pick[y, y * cols] = 1.0
        pick[SIDE + y, y * cols + cols - 1] = 1.0
    for x in range(cols - 1):
        shift[0, x, x + 1] = 1.0
        shift[1, x + 1, x] = 1.0
    for side, col in ((0, 0), (1, cols - 1)):
        spread[side, 0, rows - 1, col] = 1.0
        for y in range(rows):
            spread[side, 1, y, (y + 1) * cols + col] = 1.0
        spread[side, 2, 0, (rows + 1) * cols + col] = 1.0
    return (
        jnp.asarray(pick, BF16),
        jnp.asarray(shift, BF16),
        jnp.asarray(spread.reshape(2, 3 * SIDE, wide), BF16),
    )


def body(x, g, gain, bias, weight, filter_taps, sharpness, out_matrix):
    channels, rows, cols = x.shape
    cells = rows * cols
    width = weight.shape[0]
    texels = float(cells * lax.axis_size("gy") * lax.axis_size("gx"))
    pick, shift, spread = constants(rows, cols)
    x = x.reshape(channels, cells)
    g = g.reshape(channels, cells)
    gain, bias = gain[:, None], bias[:, None]
    taps = filter_taps.reshape(9, width).T
    shape = jax.ShapeDtypeStruct

    p, normed, stat, edge = call(
        functools.partial(front_kernel, rows, cols),
        (shape((width, cells), BF16), shape((256, cells), BF16), shape((8, cells), F32),
         shape((2 * SIDE, width), BF16)),
        (x, gain, bias, weight, pick),
    )
    top, bot, side = halo(p, edge, cols, 0)
    moved = pltpu.VMEM((2, width, (rows + 2) * cols), BF16)
    conv, part = call(
        functools.partial(conv_kernel, rows, cols),
        (shape((width, cells), BF16), shape((padded_rows(2 * (channels + HD)), 128), F32)),
        (p, top, bot, side, shift, spread, taps, g),
        scratch=(moved, pltpu.VMEM((width, 128), F32)),
    )
    total = sum_over_devices(part, 1)
    grad, edge, omap_adj, sharp_adj = call(
        functools.partial(attend_kernel, texels),
        (shape((width, cells), BF16), shape((2 * SIDE, width), BF16),
         shape((channels, channels), F32), shape((ATTENDER_TOTAL,), F32)),
        (total, sharpness, out_matrix, conv, g, pick),
        in_specs=[VMEM, SMEM] + [VMEM] * 4,
        out_specs=(VMEM, VMEM, VMEM, SMEM),
    )
    top, bot, side = halo(grad, edge, cols, 2)
    out, part = call(
        functools.partial(back_kernel, rows, cols, texels),
        (shape((channels, cells), BF16), shape((padded_rows(2 * width), 128), F32)),
        (grad, top, bot, side, shift, spread, taps, p, normed, weight, x, stat, gain, g),
        scratch=(moved, pltpu.VMEM((width, cells), BF16), pltpu.VMEM((width, 128), F32)),
    )
    total = sum_over_devices(part, 3)
    low, high = total[:width], total[width:2 * width]
    weight_adj = jnp.concatenate([low, high[:, :channels - 128]], axis=1)
    filter_adj = high[:, 64:73].T.reshape(3, 3, width)
    return (
        out.reshape(channels, rows, cols),
        weight_adj,
        filter_adj,
        omap_adj,
        sharp_adj,
        high[:channels, 73],
        high[:channels, 74],
    )


def solution(mesh):
    in_specs = (P(None, "gy", "gx"), P(None, "gy", "gx"), P(), P(), P(), P(), P(), P())
    out_specs = (P(None, "gy", "gx"), P(), P(), P(), P(), P(), P())
    return jax.shard_map(body, mesh=mesh, in_specs=in_specs, out_specs=out_specs, check_vma=False)
```

```python
import functools

import jax
import jax.numpy as jnp
import numpy as np
from jax import lax
from jax.experimental import pallas as pl
from jax.experimental.pallas import tpu as pltpu
from jax.sharding import PartitionSpec as P

ATTENDER_TOTAL = 4
HD = 48
F32 = jnp.float32
BF16 = jnp.bfloat16
MESH = pl.DeviceIdType.MESH
VMEM = pl.BlockSpec(memory_space=pltpu.VMEM)
SMEM = pl.BlockSpec(memory_space=pltpu.SMEM)
NT = (((1,), (1,)), ((), ()))
TN = (((0,), (0,)), ((), ()))
LIMIT = 56 * 1024 * 1024
SIDE = 16


def dot(a, b, dims=(((1,), (0,)), ((), ()))):
    return lax.dot_general(a, b, dims, preferred_element_type=F32)


def dot_full(a, b, dims=(((1,), (0,)), ((), ()))):
    return lax.dot_general(
        a, b, dims, preferred_element_type=F32, precision=lax.Precision.HIGHEST
    )


def to_col(row):
    size = row.shape[1]
    eye = lax.broadcasted_iota(jnp.int32, (size, size), 0) == lax.broadcasted_iota(
        jnp.int32, (size, size), 1
    )
    return jnp.sum(jnp.where(eye, row, 0.0), axis=1, keepdims=True)


def front_kernel(rows, cols, x_ref, gain_ref, bias_ref, wt_ref, sel_ref,
                 p_ref, normed_ref, stat_ref, edge_ref):
    channels = x_ref.shape[0]
    gain, bias = to_col(gain_ref[...]), to_col(bias_ref[...])
    weight = jnp.transpose(wt_ref[...])
    edge = jnp.zeros((2 * SIDE, channels), F32)
    stat_ref[...] = jnp.zeros_like(stat_ref)
    for y in range(rows):
        at = pl.ds(y * cols, cols)
        x = x_ref[:, at].astype(F32)
        mean = jnp.sum(x, axis=0, keepdims=True) / channels
        centred = x - mean
        var = jnp.sum(centred * centred, axis=0, keepdims=True) / channels
        inv = 1.0 / jnp.sqrt(var + 1e-05)
        stat_ref[pl.ds(0, 1), at] = mean
        stat_ref[pl.ds(1, 1), at] = inv
        normed = ((centred * inv) * gain + bias).astype(BF16)
        normed_ref[:, at] = normed
        p_ref[:, at] = dot(weight, normed).astype(BF16)
        edge = edge + dot(sel_ref[:, at], normed, NT)
    edge_ref[...] = dot(edge.astype(BF16), wt_ref[...]).astype(BF16)


def halo_kernel(cols, p_ref, edge_ref, top_ref, bot_ref, side_ref, send, recv):
    gy, gx = lax.axis_index("gy"), lax.axis_index("gx")
    ny, nx = lax.axis_size("gy"), lax.axis_size("gx")
    tail = p_ref.shape[1] - cols
    moves = []
    for dy in (-1, 0, 1):
        for dx in (-1, 0, 1):
            if dy or dx:
                moves.append((dy, dx))

    def there(dy, dx):
        ty, tx = gy + dy, gx + dx
        return (ty >= 0) & (ty < ny) & (tx >= 0) & (tx < nx), (ty, tx)

    barrier = pltpu.get_barrier_semaphore()
    for dy, dx in moves:
        ok, target = there(dy, dx)

        @pl.when(ok)
        def _(target=target):
            pl.semaphore_signal(barrier, inc=1, device_id=target, device_id_type=MESH)

    down = 1 + (gy > 0).astype(jnp.int32) + (gy < ny - 1).astype(jnp.int32)
    across = 1 + (gx > 0).astype(jnp.int32) + (gx < nx - 1).astype(jnp.int32)
    pl.semaphore_wait(barrier, down * across - 1)

    def copy(k, dy, dx, target):
        if dx == 0:
            src = p_ref.at[:, pl.ds(0 if dy < 0 else tail, cols)]
            dst = bot_ref if dy < 0 else top_ref
        else:
            src = edge_ref.at[pl.ds(0 if dx < 0 else SIDE, SIDE)]
            dst = side_ref.at[1 if dx < 0 else 0, 1 - dy]
        return pltpu.make_async_remote_copy(
            src_ref=src, dst_ref=dst, send_sem=send.at[k], recv_sem=recv.at[k],
            device_id=target, device_id_type=MESH,
        )

    for k, (dy, dx) in enumerate(moves):
        ok, target = there(dy, dx)

        @pl.when(ok)
        def _(k=k, dy=dy, dx=dx, target=target):
            copy(k, dy, dx, target).start()

    for k, (dy, dx) in enumerate(moves):
        ok, target = there(-dy, -dx)
        back, other = there(dy, dx)

        @pl.when(ok)
        def _(k=k, dy=dy, dx=dx, target=target):
            copy(k, dy, dx, target).wait_recv()

        @pl.when(jnp.logical_not(ok))
        def _(k=k, dy=dy, dx=dx):
            if dx == 0:
                ref = bot_ref if dy < 0 else top_ref
                ref[...] = jnp.zeros_like(ref)
            else:
                side_ref[1 if dx < 0 else 0, 1 - dy] = jnp.zeros(side_ref.shape[2:], BF16)

        @pl.when(back)
        def _(k=k, dy=dy, dx=dx, other=other):
            copy(k, dy, dx, other).wait_send()


def halo(p, edge, cols, collective_id):
    width = p.shape[0]
    return pl.pallas_call(
        functools.partial(halo_kernel, cols),
        out_shape=(
            jax.ShapeDtypeStruct((width, cols), BF16),
            jax.ShapeDtypeStruct((width, cols), BF16),
            jax.ShapeDtypeStruct((2, 3, SIDE, width), BF16),
        ),
        in_specs=[VMEM] * 2,
        out_specs=(VMEM,) * 3,
        scratch_shapes=[pltpu.SemaphoreType.DMA((8,)), pltpu.SemaphoreType.DMA((8,))],
        compiler_params=pltpu.CompilerParams(
            collective_id=collective_id, has_side_effects=True, vmem_limit_bytes=LIMIT
        ),
    )(p, edge)


def shift_rows(rows, cols, p_ref, top_ref, bot_ref, side_ref, shift_ref, spread_ref, moved):
    width = p_ref.shape[0]
    edges = [jnp.transpose(side_ref[side].reshape(3 * SIDE, width)) for side in range(2)]
    for y in range(rows + 2):
        if y == 0:
            row = top_ref[...]
        elif y == rows + 1:
            row = bot_ref[...]
        else:
            row = p_ref[:, pl.ds((y - 1) * cols, cols)]
        for side in range(2):
            near, far = (0, 128) if side == 0 else (cols - 128, 0)
            out = dot(row, shift_ref[side])
            at = pl.ds(y * cols + near, 128)
            fill = dot(edges[side], spread_ref[side, :, at])
            moved[side, :, at] = (out[:, near:near + 128] + fill).astype(BF16)
            rest = cols - 128
            moved[side, :, pl.ds(y * cols + far, rest)] = out[:, far:far + rest].astype(BF16)


def conv_kernel(rows, cols, p_ref, top_ref, bot_ref, side_ref, shift_ref, spread_ref, taps_ref,
                g_ref, conv_ref, part_ref, moved, squares):
    width = p_ref.shape[0]
    channels = width // 3
    part_rows = part_ref.shape[0]
    shift_rows(rows, cols, p_ref, top_ref, bot_ref, side_ref, shift_ref, spread_ref, moved)

    def chunk(i, carry):
        rs = pl.ds(pl.multiple_of(i * 16, 16), 16)
        taps = [jnp.broadcast_to(taps_ref[rs, pl.ds(k, 1)], (16, 128)) for k in range(9)]
        total = jnp.zeros((16, 128), F32)
        for half in range(cols // 128):
            got = {}
            for y in range(rows + 2):
                at = pl.ds(y * cols + half * 128, 128)
                if y == 0:
                    mid = top_ref[rs, pl.ds(half * 128, 128)]
                elif y == rows + 1:
                    mid = bot_ref[rs, pl.ds(half * 128, 128)]
                else:
                    mid = p_ref[rs, pl.ds((y - 1) * cols + half * 128, 128)]
                got[y] = (moved[0, rs, at].astype(F32), mid.astype(F32), moved[1, rs, at].astype(F32))
                if y >= 2:
                    out = jnp.zeros((16, 128), F32)
                    for a in range(3):
                        for b in range(3):
                            out = out + taps[3 * a + b] * got[y - 2 + a][b]
                    out = out.astype(BF16)
                    conv_ref[rs, pl.ds((y - 2) * cols + half * 128, 128)] = out
                    out = out.astype(F32)
                    total = total + out * out
        squares[rs, :] = jnp.broadcast_to(jnp.sum(total, axis=1, keepdims=True), (16, 128))
        return carry

    lax.fori_loop(0, width // 16, chunk, 0)
    queries = conv_ref[pl.ds(0, channels), :]
    keys = conv_ref[pl.ds(channels, channels), :]
    values = conv_ref[pl.ds(2 * channels, channels), :]
    gram = dot(queries, keys, NT)
    mixed = dot(g_ref[...], values, NT)
    lane = lax.broadcasted_iota(jnp.int32, (HD, channels), 1) // HD
    compact = jnp.zeros((HD, channels), F32)
    for h in range(channels // HD):
        compact = compact + jnp.where(lane == h, gram[h * HD:(h + 1) * HD, :], 0.0)
    pad = jnp.zeros((channels, 256 - channels), F32)
    lanes = lax.broadcasted_iota(jnp.int32, (channels, 128), 1)
    high = jnp.concatenate([mixed[:, 128:], pad], axis=1)
    high = jnp.where(lanes == 64, squares[pl.ds(0, channels), :], high)
    high = jnp.where(lanes == 65, squares[pl.ds(channels, channels), :], high)
    span = channels + HD
    part_ref[pl.ds(0, channels), :] = mixed[:, :128]
    part_ref[pl.ds(channels, HD), :] = compact[:, :128]
    part_ref[pl.ds(span, channels), :] = high
    part_ref[pl.ds(span + channels, HD), :] = jnp.concatenate(
        [compact[:, 128:], pad[:HD]], axis=1
    )
    part_ref[pl.ds(2 * span, part_rows - 2 * span), :] = jnp.zeros((part_rows - 2 * span, 128), F32)


def sum_kernel(finish, in_ref, *refs):
    results, (out_ref, got_x, held, got_y, send, recv) = refs[:-6], refs[-6:]
    gy, gx = lax.axis_index("gy"), lax.axis_index("gx")
    ny, nx = lax.axis_size("gy"), lax.axis_size("gx")
    barrier = pltpu.get_barrier_semaphore()
    for d in range(1, nx):
        pl.semaphore_signal(barrier, inc=1, device_id=(gy, lax.rem(gx + d, nx)), device_id_type=MESH)
    for d in range(1, ny):
        pl.semaphore_signal(barrier, inc=1, device_id=(lax.rem(gy + d, ny), gx), device_id_type=MESH)
    pl.semaphore_wait(barrier, nx + ny - 2)

    slot = 0

    def exchange(copies):
        nonlocal slot
        made = []
        for src, dst, target in copies:
            made.append(pltpu.make_async_remote_copy(
                src_ref=src, dst_ref=dst, send_sem=send.at[slot], recv_sem=recv.at[slot],
                device_id=target, device_id_type=MESH,
            ))
            slot += 1
            made[-1].start()
        for copy in made:
            copy.wait()

    exchange([
        (in_ref.at[lax.rem(gx + d, nx)], got_x.at[d - 1], (gy, lax.rem(gx + d, nx)))
        for d in range(1, nx)
    ])
    total = in_ref[gx].astype(F32)
    for d in range(1, nx):
        total = total + got_x[d - 1].astype(F32)
    held[...] = total.astype(held.dtype)
    exchange([
        (held.at[lax.rem(gy + d, ny)], got_y.at[d - 1], (lax.rem(gy + d, ny), gx))
        for d in range(1, ny)
    ])
    total = held[gy].astype(F32)
    for d in range(1, ny):
        total = total + got_y[d - 1].astype(F32)
    out_ref[gx, gy] = total.astype(out_ref.dtype)
    exchange([
        (out_ref.at[gx, gy], out_ref.at[gx, gy], (lax.rem(gy + d, ny), gx)) for d in range(1, ny)
    ])
    exchange([
        (out_ref.at[gx], out_ref.at[gx], (gy, lax.rem(gx + d, nx))) for d in range(1, nx)
    ])
    finish(out_ref[...].reshape(-1, 128), *results)


def whole_sum(total, out_ref):
    out_ref[...] = total


def parameter_sums(total, weight_ref, taps_ref, gain_ref, bias_ref):
    total = total.astype(F32)
    channels, width = weight_ref.shape
    whole, half, at = width // 128, channels // 2, 0
    for i in range(whole):
        weight_ref[:, pl.ds(i * 128, 128)] = total[at:at + channels]
        at += channels
    rest = total[at:at + half]
    left = width - whole * 128
    weight_ref[:, pl.ds(whole * 128, left)] = jnp.concatenate([rest[:, :left], rest[:, left:]], axis=0)
    at += half
    small = jnp.concatenate([total[at + 16 * i:at + 16 * i + 16] for i in range(whole + 1)], axis=1)
    taps_ref[...] = small[:9, :width]
    gain_ref[...] = small[9:10, :channels]
    bias_ref[...] = small[10:11, :channels]


def sum_over_devices(part, collective_id, finish, out_shape):
    ny, nx = lax.axis_size("gy"), lax.axis_size("gx")
    piece = part.shape[0] // (nx * ny)
    count = 2 * (nx + ny - 2)
    shape = (nx, ny, piece, 128)
    return pl.pallas_call(
        functools.partial(sum_kernel, finish),
        out_shape=out_shape,
        in_specs=[VMEM],
        out_specs=(VMEM,) * len(out_shape),
        scratch_shapes=[
            pltpu.VMEM(shape, part.dtype),
            pltpu.VMEM((nx - 1, ny, piece, 128), part.dtype),
            pltpu.VMEM((ny, piece, 128), part.dtype),
            pltpu.VMEM((ny - 1, piece, 128), part.dtype),
            pltpu.SemaphoreType.DMA((count,)),
            pltpu.SemaphoreType.DMA((count,)),
        ],
        compiler_params=pltpu.CompilerParams(
            collective_id=collective_id, has_side_effects=True, vmem_limit_bytes=LIMIT
        ),
    )(part.reshape(shape))


def padded_rows(count, tile=8):
    unit = tile * lax.axis_size("gy") * lax.axis_size("gx")
    return -(-count // unit) * unit


def attend_kernel(texels, tot_ref, sharp_ref, wo_ref, conv_ref, g_ref, sel_ref,
                  grad_ref, edge_ref, omap_ref, sharp_adj_ref):
    channels = wo_ref.shape[0]
    span = channels + HD
    low, high = tot_ref[pl.ds(0, channels), :], tot_ref[pl.ds(span, channels), :]
    mixed = jnp.concatenate([low, high[:, :channels - 128]], axis=1)
    sq, sk = high[:, 64:65], high[:, 65:66]
    compact = jnp.concatenate(
        [tot_ref[pl.ds(channels, HD), :], tot_ref[pl.ds(span + channels, HD), :][:, :channels - 128]],
        axis=1,
    )
    heads = channels // HD
    gram = jnp.concatenate([compact] * heads, axis=0)
    rows = lax.broadcasted_iota(jnp.int32, (channels, channels), 0)
    lanes = lax.broadcasted_iota(jnp.int32, (channels, channels), 1)
    same = (rows // HD) == (lanes // HD)
    eye = rows == lanes
    head = lax.broadcasted_iota(jnp.int32, (channels, 1), 0) // HD
    sharp = jnp.zeros((channels, 1), F32)
    for h in range(heads):
        sharp = jnp.where(head == h, sharp_ref[h], sharp)

    def to_row(col):
        return jnp.sum(jnp.where(eye, col, 0.0), axis=0, keepdims=True)

    norms = jnp.sqrt(sq + 1e-06) * jnp.sqrt(to_row(sk) + 1e-06)
    logits = jnp.where(same, sharp * gram / norms, 0.0)
    expo = jnp.where(same, jnp.exp(logits), 0.0)
    attend = expo / jnp.sum(expo, axis=1, keepdims=True)
    attend_low = attend.astype(BF16)
    omap_ref[...] = dot_full(mixed, attend_low.astype(F32), NT) / texels
    grad_attend = dot_full(wo_ref[...].astype(F32), mixed, TN)
    grad_logits = attend * (grad_attend - jnp.sum(attend * grad_attend, axis=1, keepdims=True))
    product = grad_logits * logits
    row_terms = jnp.sum(product, axis=1, keepdims=True)
    col_terms = to_col(jnp.sum(product, axis=0, keepdims=True))
    for h in range(heads):
        sharp_adj_ref[h] = jnp.sum(jnp.where(head == h, row_terms, 0.0)) / sharp_ref[h] / texels
    coupling = (sharp * grad_logits / norms).astype(BF16)
    row_scale = row_terms / (sq + 1e-06)
    col_scale = col_terms / (sk + 1e-06)
    cells = conv_ref.shape[1]
    step = 256
    edges = [jnp.zeros((2 * SIDE, channels), F32) for _ in range(3)]
    for n in range(cells // step):
        at = pl.ds(n * step, step)
        queries = conv_ref[pl.ds(0, channels), at]
        keys = conv_ref[pl.ds(channels, channels), at]
        grad_attended = dot(wo_ref[...], g_ref[:, at], TN).astype(BF16)
        grads = (
            dot(coupling, keys) - row_scale * queries.astype(F32),
            dot(coupling, queries, TN) - col_scale * keys.astype(F32),
            dot(attend_low, grad_attended, TN),
        )
        for i, grad in enumerate(grads):
            grad = grad.astype(BF16)
            grad_ref[pl.ds(i * channels, channels), at] = grad
            edges[i] = edges[i] + dot(sel_ref[:, at], grad, NT)
    edge_ref[...] = jnp.concatenate(edges, axis=1).astype(BF16)


def back_kernel(rows, cols, texels, grad_ref, top_ref, bot_ref, side_ref, shift_ref, spread_ref,
                taps_ref, p_ref, normed_ref, wt_ref, x_ref, stat_ref, gain_ref, g_ref,
                out_ref, part_ref, moved, gp_ref, sums):
    width = grad_ref.shape[0]
    channels = width // 3
    part_rows = part_ref.shape[0]
    shift_rows(rows, cols, grad_ref, top_ref, bot_ref, side_ref, shift_ref, spread_ref, moved)

    def chunk(i, carry):
        rs = pl.ds(pl.multiple_of(i * 16, 16), 16)
        taps = [jnp.broadcast_to(taps_ref[rs, pl.ds(k, 1)], (16, 128)) for k in range(9)]
        tap_sums = [jnp.zeros((16, 128), F32) for _ in range(9)]
        for half in range(cols // 128):
            got = {}
            for y in range(rows + 2):
                at = pl.ds(y * cols + half * 128, 128)
                if y == 0:
                    mid = top_ref[rs, pl.ds(half * 128, 128)]
                elif y == rows + 1:
                    mid = bot_ref[rs, pl.ds(half * 128, 128)]
                else:
                    mid = grad_ref[rs, pl.ds((y - 1) * cols + half * 128, 128)]
                got[y] = (moved[0, rs, at].astype(F32), mid.astype(F32), moved[1, rs, at].astype(F32))
                if y >= 2:
                    here = pl.ds((y - 2) * cols + half * 128, 128)
                    field = p_ref[rs, here].astype(F32)
                    out = jnp.zeros((16, 128), F32)
                    for a in range(3):
                        for b in range(3):
                            k = 3 * (2 - a) + (2 - b)
                            out = out + taps[k] * got[y - 2 + a][b]
                            tap_sums[k] = tap_sums[k] + field * got[y - 2 + a][b]
                    gp_ref[rs, here] = out.astype(BF16)
        lane = lax.broadcasted_iota(jnp.int32, (16, 128), 1)
        packed = jnp.zeros((16, 128), F32)
        for k in range(9):
            packed = jnp.where(lane == k, jnp.sum(tap_sums[k], axis=1, keepdims=True), packed)
        sums[rs, :] = packed
        return carry

    lax.fori_loop(0, width // 16, chunk, 0)
    gain = to_col(gain_ref[...])
    gain_sum = jnp.zeros((channels, cols), F32)
    bias_sum = jnp.zeros((channels, cols), F32)
    for y in range(rows):
        at = pl.ds(y * cols, cols)
        grad_normed = dot(wt_ref[...], gp_ref[:, at])
        mean, inv = stat_ref[pl.ds(0, 1), at], stat_ref[pl.ds(1, 1), at]
        x_hat = (x_ref[:, at].astype(F32) - mean) * inv
        gain_sum = gain_sum + grad_normed * x_hat
        bias_sum = bias_sum + grad_normed
        grad_hat = grad_normed * gain
        centre = jnp.sum(grad_hat, axis=0, keepdims=True) / channels
        slope = jnp.sum(grad_hat * x_hat, axis=0, keepdims=True) / channels
        out = g_ref[:, at].astype(F32) + inv * (grad_hat - centre - x_hat * slope)
        out_ref[:, at] = out.astype(BF16)
    lane = lax.broadcasted_iota(jnp.int32, (channels, 128), 1)
    first = sums[pl.ds(0, channels), :]
    first = jnp.where(lane == 9, jnp.sum(gain_sum, axis=1, keepdims=True), first)
    first = jnp.where(lane == 10, jnp.sum(bias_sum, axis=1, keepdims=True), first)
    sums[pl.ds(0, channels), :] = first
    sums[pl.ds(width, 64), :] = jnp.zeros((64, 128), F32)
    weight = dot(normed_ref[...], gp_ref[...], NT) / texels
    whole, half, at = width // 128, channels // 2, 0
    for i in range(whole):
        part_ref[pl.ds(at, channels), :] = weight[:, i * 128:(i + 1) * 128].astype(BF16)
        at += channels
    rest = weight[:, whole * 128:]
    part_ref[pl.ds(at, half), :] = jnp.concatenate([rest[:half], rest[half:]], axis=1).astype(BF16)
    at += half
    for i in range(whole + 1):
        block = jnp.transpose(sums[pl.ds(i * 128, 128), :])[:16]
        part_ref[pl.ds(at, 16), :] = (block / texels).astype(BF16)
        at += 16
    part_ref[pl.ds(at, part_rows - at), :] = jnp.zeros((part_rows - at, 128), BF16)


def call(kernel, out_shape, args, in_specs=None, out_specs=None, scratch=()):
    return pl.pallas_call(
        kernel,
        out_shape=out_shape,
        in_specs=in_specs or [VMEM] * len(args),
        out_specs=out_specs or (VMEM,) * len(out_shape),
        scratch_shapes=scratch,
        compiler_params=pltpu.CompilerParams(vmem_limit_bytes=LIMIT),
    )(*args)


def constants(rows, cols):
    cells, wide = rows * cols, (rows + 2) * cols
    pick = np.zeros((2 * SIDE, cells), np.float32)
    shift = np.zeros((2, cols, cols), np.float32)
    spread = np.zeros((2, 3, SIDE, wide), np.float32)
    for y in range(rows):
        pick[y, y * cols] = 1.0
        pick[SIDE + y, y * cols + cols - 1] = 1.0
    for x in range(cols - 1):
        shift[0, x, x + 1] = 1.0
        shift[1, x + 1, x] = 1.0
    for side, col in ((0, 0), (1, cols - 1)):
        spread[side, 0, rows - 1, col] = 1.0
        for y in range(rows):
            spread[side, 1, y, (y + 1) * cols + col] = 1.0
        spread[side, 2, 0, (rows + 1) * cols + col] = 1.0
    return (
        jnp.asarray(pick, BF16),
        jnp.asarray(shift, BF16),
        jnp.asarray(spread.reshape(2, 3 * SIDE, wide), BF16),
    )


def body(x, g, gain, bias, weight, filter_taps, sharpness, out_matrix):
    channels, rows, cols = x.shape
    cells = rows * cols
    width = weight.shape[0]
    texels = float(cells * lax.axis_size("gy") * lax.axis_size("gx"))
    pick, shift, spread = constants(rows, cols)
    x = x.reshape(channels, cells)
    g = g.reshape(channels, cells)
    gain, bias, weight_t = gain[None, :], bias[None, :], weight.T
    taps = filter_taps.reshape(9, width).T
    shape = jax.ShapeDtypeStruct

    p, normed, stat, edge = call(
        functools.partial(front_kernel, rows, cols),
        (shape((width, cells), BF16), shape((channels, cells), BF16), shape((8, cells), F32),
         shape((2 * SIDE, width), BF16)),
        (x, gain, bias, weight_t, pick),
    )
    top, bot, side = halo(p, edge, cols, 0)
    moved = pltpu.VMEM((2, width, (rows + 2) * cols), BF16)
    conv, part = call(
        functools.partial(conv_kernel, rows, cols),
        (shape((width, cells), BF16), shape((padded_rows(2 * (channels + HD)), 128), F32)),
        (p, top, bot, side, shift, spread, taps, g),
        scratch=(moved, pltpu.VMEM((width, 128), F32)),
    )
    (total,) = sum_over_devices(part, 1, whole_sum, (shape(part.shape, F32),))
    grad, edge, omap_adj, sharp_adj = call(
        functools.partial(attend_kernel, texels),
        (shape((width, cells), BF16), shape((2 * SIDE, width), BF16),
         shape((channels, channels), F32), shape((ATTENDER_TOTAL,), F32)),
        (total, sharpness, out_matrix, conv, g, pick),
        in_specs=[VMEM, SMEM] + [VMEM] * 4,
        out_specs=(VMEM, VMEM, VMEM, SMEM),
    )
    top, bot, side = halo(grad, edge, cols, 2)
    part_rows = width // 128 * channels + channels // 2 + (width // 128 + 1) * 16
    out, part = call(
        functools.partial(back_kernel, rows, cols, texels),
        (shape((channels, cells), BF16), shape((padded_rows(part_rows, 16), 128), BF16)),
        (grad, top, bot, side, shift, spread, taps, p, normed, weight_t, x, stat, gain, g),
        scratch=(moved, pltpu.VMEM((width, cells), BF16), pltpu.VMEM((width + 64, 128), F32)),
    )
    weight_adj, filter_adj, gain_adj, bias_adj = sum_over_devices(
        part, 3, parameter_sums,
        (shape((channels, width), F32), shape((9, width), F32),
         shape((1, channels), F32), shape((1, channels), F32)),
    )
    return (
        out.reshape(channels, rows, cols),
        weight_adj.T,
        filter_adj.reshape(3, 3, width),
        omap_adj,
        sharp_adj,
        gain_adj.reshape(channels),
        bias_adj.reshape(channels),
    )


def solution(mesh):
    in_specs = (P(None, "gy", "gx"), P(None, "gy", "gx"), P(), P(), P(), P(), P(), P())
    out_specs = (P(None, "gy", "gx"), P(), P(), P(), P(), P(), P())
    return jax.shard_map(body, mesh=mesh, in_specs=in_specs, out_specs=out_specs, check_vma=False)
```

```python
import functools

import jax
import jax.numpy as jnp
import numpy as np
from jax import lax
from jax.experimental import pallas as pl
from jax.experimental.pallas import tpu as pltpu
from jax.sharding import PartitionSpec as P

ATTENDER_TOTAL = 4
HD = 48
F32 = jnp.float32
BF16 = jnp.bfloat16
MESH = pl.DeviceIdType.MESH
VMEM = pl.BlockSpec(memory_space=pltpu.VMEM)
SMEM = pl.BlockSpec(memory_space=pltpu.SMEM)
NT = (((1,), (1,)), ((), ()))
TN = (((0,), (0,)), ((), ()))
LIMIT = 56 * 1024 * 1024
SIDE = 16


def dot(a, b, dims=(((1,), (0,)), ((), ()))):
    return lax.dot_general(a, b, dims, preferred_element_type=F32)


def dot_full(a, b, dims=(((1,), (0,)), ((), ()))):
    return lax.dot_general(
        a, b, dims, preferred_element_type=F32, precision=lax.Precision.HIGHEST
    )


def to_col(row):
    size = row.shape[1]
    eye = lax.broadcasted_iota(jnp.int32, (size, size), 0) == lax.broadcasted_iota(
        jnp.int32, (size, size), 1
    )
    return jnp.sum(jnp.where(eye, row, 0.0), axis=1, keepdims=True)


def front_kernel(rows, cols, x_ref, gain_ref, bias_ref, wt_ref, sel_ref,
                 p_ref, normed_ref, stat_ref, edge_ref):
    channels = x_ref.shape[0]
    gain, bias = to_col(gain_ref[...]), to_col(bias_ref[...])
    weight = jnp.transpose(wt_ref[...])
    edge = jnp.zeros((2 * SIDE, channels), F32)
    stat_ref[...] = jnp.zeros_like(stat_ref)
    for y in range(rows):
        at = pl.ds(y * cols, cols)
        x = x_ref[:, at].astype(F32)
        mean = jnp.sum(x, axis=0, keepdims=True) / channels
        centred = x - mean
        var = jnp.sum(centred * centred, axis=0, keepdims=True) / channels
        inv = 1.0 / jnp.sqrt(var + 1e-05)
        stat_ref[pl.ds(0, 1), at] = mean
        stat_ref[pl.ds(1, 1), at] = inv
        normed = ((centred * inv) * gain + bias).astype(BF16)
        normed_ref[:, at] = normed
        p_ref[:, at] = dot(weight, normed).astype(BF16)
        edge = edge + dot(sel_ref[:, at], normed, NT)
    edge_ref[...] = dot(edge.astype(BF16), wt_ref[...]).astype(BF16)


def halo_kernel(cols, p_ref, edge_ref, top_ref, bot_ref, side_ref, send, recv):
    gy, gx = lax.axis_index("gy"), lax.axis_index("gx")
    ny, nx = lax.axis_size("gy"), lax.axis_size("gx")
    tail = p_ref.shape[1] - cols
    moves = []
    for dy in (-1, 0, 1):
        for dx in (-1, 0, 1):
            if dy or dx:
                moves.append((dy, dx))

    def there(dy, dx):
        ty, tx = gy + dy, gx + dx
        return (ty >= 0) & (ty < ny) & (tx >= 0) & (tx < nx), (ty, tx)

    barrier = pltpu.get_barrier_semaphore()
    for dy, dx in moves:
        ok, target = there(dy, dx)

        @pl.when(ok)
        def _(target=target):
            pl.semaphore_signal(barrier, inc=1, device_id=target, device_id_type=MESH)

    down = 1 + (gy > 0).astype(jnp.int32) + (gy < ny - 1).astype(jnp.int32)
    across = 1 + (gx > 0).astype(jnp.int32) + (gx < nx - 1).astype(jnp.int32)
    pl.semaphore_wait(barrier, down * across - 1)

    def copy(k, dy, dx, target):
        if dx == 0:
            src = p_ref.at[:, pl.ds(0 if dy < 0 else tail, cols)]
            dst = bot_ref if dy < 0 else top_ref
        else:
            src = edge_ref.at[pl.ds(0 if dx < 0 else SIDE, SIDE)]
            dst = side_ref.at[1 if dx < 0 else 0, 1 - dy]
        return pltpu.make_async_remote_copy(
            src_ref=src, dst_ref=dst, send_sem=send.at[k], recv_sem=recv.at[k],
            device_id=target, device_id_type=MESH,
        )

    for k, (dy, dx) in enumerate(moves):
        ok, target = there(dy, dx)

        @pl.when(ok)
        def _(k=k, dy=dy, dx=dx, target=target):
            copy(k, dy, dx, target).start()

    for k, (dy, dx) in enumerate(moves):
        ok, target = there(-dy, -dx)
        back, other = there(dy, dx)

        @pl.when(ok)
        def _(k=k, dy=dy, dx=dx, target=target):
            copy(k, dy, dx, target).wait_recv()

        @pl.when(jnp.logical_not(ok))
        def _(k=k, dy=dy, dx=dx):
            if dx == 0:
                ref = bot_ref if dy < 0 else top_ref
                ref[...] = jnp.zeros_like(ref)
            else:
                side_ref[1 if dx < 0 else 0, 1 - dy] = jnp.zeros(side_ref.shape[2:], BF16)

        @pl.when(back)
        def _(k=k, dy=dy, dx=dx, other=other):
            copy(k, dy, dx, other).wait_send()


def halo(p, edge, cols, collective_id):
    width = p.shape[0]
    return pl.pallas_call(
        functools.partial(halo_kernel, cols),
        out_shape=(
            jax.ShapeDtypeStruct((width, cols), BF16),
            jax.ShapeDtypeStruct((width, cols), BF16),
            jax.ShapeDtypeStruct((2, 3, SIDE, width), BF16),
        ),
        in_specs=[VMEM] * 2,
        out_specs=(VMEM,) * 3,
        scratch_shapes=[pltpu.SemaphoreType.DMA((8,)), pltpu.SemaphoreType.DMA((8,))],
        compiler_params=pltpu.CompilerParams(
            collective_id=collective_id, has_side_effects=True, vmem_limit_bytes=LIMIT
        ),
    )(p, edge)


def shift_rows(rows, cols, p_ref, top_ref, bot_ref, side_ref, shift_ref, spread_ref, moved):
    width = p_ref.shape[0]
    edges = [jnp.transpose(side_ref[side].reshape(3 * SIDE, width)) for side in range(2)]
    for y in range(rows + 2):
        if y == 0:
            row = top_ref[...]
        elif y == rows + 1:
            row = bot_ref[...]
        else:
            row = p_ref[:, pl.ds((y - 1) * cols, cols)]
        for side in range(2):
            near, far = (0, 128) if side == 0 else (cols - 128, 0)
            out = dot(row, shift_ref[side])
            at = pl.ds(y * cols + near, 128)
            fill = dot(edges[side], spread_ref[side, :, at])
            moved[side, :, at] = (out[:, near:near + 128] + fill).astype(BF16)
            rest = cols - 128
            moved[side, :, pl.ds(y * cols + far, rest)] = out[:, far:far + rest].astype(BF16)


def conv_kernel(rows, cols, p_ref, top_ref, bot_ref, side_ref, shift_ref, spread_ref, taps_ref,
                g_ref, conv_ref, part_ref, moved, squares):
    width = p_ref.shape[0]
    channels = width // 3
    part_rows = part_ref.shape[0]
    shift_rows(rows, cols, p_ref, top_ref, bot_ref, side_ref, shift_ref, spread_ref, moved)

    def chunk(i, carry):
        rs = pl.ds(pl.multiple_of(i * 16, 16), 16)
        taps = [jnp.broadcast_to(taps_ref[rs, pl.ds(k, 1)], (16, 128)) for k in range(9)]
        total = jnp.zeros((16, 128), F32)
        for half in range(cols // 128):
            got = {}
            for y in range(rows + 2):
                at = pl.ds(y * cols + half * 128, 128)
                if y == 0:
                    mid = top_ref[rs, pl.ds(half * 128, 128)]
                elif y == rows + 1:
                    mid = bot_ref[rs, pl.ds(half * 128, 128)]
                else:
                    mid = p_ref[rs, pl.ds((y - 1) * cols + half * 128, 128)]
                got[y] = (moved[0, rs, at].astype(F32), mid.astype(F32), moved[1, rs, at].astype(F32))
                if y >= 2:
                    out = jnp.zeros((16, 128), F32)
                    for a in range(3):
                        for b in range(3):
                            out = out + taps[3 * a + b] * got[y - 2 + a][b]
                    out = out.astype(BF16)
                    conv_ref[rs, pl.ds((y - 2) * cols + half * 128, 128)] = out
                    out = out.astype(F32)
                    total = total + out * out
        squares[rs, :] = jnp.broadcast_to(jnp.sum(total, axis=1, keepdims=True), (16, 128))
        return carry

    lax.fori_loop(0, width // 16, chunk, 0)
    queries = conv_ref[pl.ds(0, channels), :]
    keys = conv_ref[pl.ds(channels, channels), :]
    values = conv_ref[pl.ds(2 * channels, channels), :]
    gram = dot(queries, keys, NT)
    mixed = dot(g_ref[...], values, NT)
    lane = lax.broadcasted_iota(jnp.int32, (HD, channels), 1) // HD
    compact = jnp.zeros((HD, channels), F32)
    for h in range(channels // HD):
        compact = compact + jnp.where(lane == h, gram[h * HD:(h + 1) * HD, :], 0.0)
    pad = jnp.zeros((channels, 256 - channels), F32)
    lanes = lax.broadcasted_iota(jnp.int32, (channels, 128), 1)
    high = jnp.concatenate([mixed[:, 128:], pad], axis=1)
    high = jnp.where(lanes == 64, squares[pl.ds(0, channels), :], high)
    high = jnp.where(lanes == 65, squares[pl.ds(channels, channels), :], high)
    span = channels + HD
    part_ref[pl.ds(0, channels), :] = mixed[:, :128]
    part_ref[pl.ds(channels, HD), :] = compact[:, :128]
    part_ref[pl.ds(span, channels), :] = high
    part_ref[pl.ds(span + channels, HD), :] = jnp.concatenate(
        [compact[:, 128:], pad[:HD]], axis=1
    )
    part_ref[pl.ds(2 * span, part_rows - 2 * span), :] = jnp.zeros((part_rows - 2 * span, 128), F32)


def sum_kernel(finish, in_ref, *refs):
    results, (out_ref, got_x, held, got_y, send, recv) = refs[:-6], refs[-6:]
    gy, gx = lax.axis_index("gy"), lax.axis_index("gx")
    ny, nx = lax.axis_size("gy"), lax.axis_size("gx")
    barrier = pltpu.get_barrier_semaphore()
    for d in range(1, nx):
        pl.semaphore_signal(barrier, inc=1, device_id=(gy, lax.rem(gx + d, nx)), device_id_type=MESH)
    for d in range(1, ny):
        pl.semaphore_signal(barrier, inc=1, device_id=(lax.rem(gy + d, ny), gx), device_id_type=MESH)
    pl.semaphore_wait(barrier, nx + ny - 2)

    slot = 0

    def exchange(copies):
        nonlocal slot
        made = []
        for src, dst, target in copies:
            made.append(pltpu.make_async_remote_copy(
                src_ref=src, dst_ref=dst, send_sem=send.at[slot], recv_sem=recv.at[slot],
                device_id=target, device_id_type=MESH,
            ))
            slot += 1
            made[-1].start()
        for copy in made:
            copy.wait()

    exchange([
        (in_ref.at[lax.rem(gx + d, nx)], got_x.at[d - 1], (gy, lax.rem(gx + d, nx)))
        for d in range(1, nx)
    ])
    total = in_ref[gx].astype(F32)
    for d in range(1, nx):
        total = total + got_x[d - 1].astype(F32)
    held[...] = total.astype(held.dtype)
    exchange([
        (held.at[lax.rem(gy + d, ny)], got_y.at[d - 1], (lax.rem(gy + d, ny), gx))
        for d in range(1, ny)
    ])
    total = held[gy].astype(F32)
    for d in range(1, ny):
        total = total + got_y[d - 1].astype(F32)
    out_ref[gx, gy] = total.astype(out_ref.dtype)
    exchange([
        (out_ref.at[gx, gy], out_ref.at[gx, gy], (lax.rem(gy + d, ny), gx)) for d in range(1, ny)
    ])
    exchange([
        (out_ref.at[gx], out_ref.at[gx], (gy, lax.rem(gx + d, nx))) for d in range(1, nx)
    ])
    finish(out_ref[...].reshape(-1, 128), *results)


def whole_sum(total, out_ref):
    out_ref[...] = total


def parameter_kernel(total_ref, weight_ref, taps_ref, gain_ref, bias_ref):
    total = total_ref[...].astype(F32)
    channels, width = weight_ref.shape
    whole, half, at = width // 128, channels // 2, 0
    for i in range(whole):
        weight_ref[:, pl.ds(i * 128, 128)] = total[at:at + channels]
        at += channels
    rest = total[at:at + half]
    left = width - whole * 128
    weight_ref[:, pl.ds(whole * 128, left)] = jnp.concatenate([rest[:, :left], rest[:, left:]], axis=0)
    at += half
    small = jnp.concatenate([total[at + 16 * i:at + 16 * i + 16] for i in range(whole + 1)], axis=1)
    for a in range(3):
        taps_ref[a] = small[3 * a:3 * a + 3, :width]
    gain_ref[...] = small[9:10, :channels]
    bias_ref[...] = small[10:11, :channels]


def sum_over_devices(part, collective_id, finish, out_shape):
    ny, nx = lax.axis_size("gy"), lax.axis_size("gx")
    piece = part.shape[0] // (nx * ny)
    count = 2 * (nx + ny - 2)
    shape = (nx, ny, piece, 128)
    return pl.pallas_call(
        functools.partial(sum_kernel, finish),
        out_shape=out_shape,
        in_specs=[VMEM],
        out_specs=(VMEM,) * len(out_shape),
        scratch_shapes=[
            pltpu.VMEM(shape, part.dtype),
            pltpu.VMEM((nx - 1, ny, piece, 128), part.dtype),
            pltpu.VMEM((ny, piece, 128), part.dtype),
            pltpu.VMEM((ny - 1, piece, 128), part.dtype),
            pltpu.SemaphoreType.DMA((count,)),
            pltpu.SemaphoreType.DMA((count,)),
        ],
        compiler_params=pltpu.CompilerParams(
            collective_id=collective_id, has_side_effects=True, vmem_limit_bytes=LIMIT
        ),
    )(part.reshape(shape))


def padded_rows(count, tile=8):
    unit = tile * lax.axis_size("gy") * lax.axis_size("gx")
    return -(-count // unit) * unit


def attend_kernel(texels, tot_ref, sharp_ref, wo_ref, conv_ref, g_ref, sel_ref,
                  grad_ref, edge_ref, omap_ref, sharp_adj_ref):
    channels = wo_ref.shape[0]
    span = channels + HD
    low, high = tot_ref[pl.ds(0, channels), :], tot_ref[pl.ds(span, channels), :]
    mixed = jnp.concatenate([low, high[:, :channels - 128]], axis=1)
    sq, sk = high[:, 64:65], high[:, 65:66]
    compact = jnp.concatenate(
        [tot_ref[pl.ds(channels, HD), :], tot_ref[pl.ds(span + channels, HD), :][:, :channels - 128]],
        axis=1,
    )
    heads = channels // HD
    gram = jnp.concatenate([compact] * heads, axis=0)
    rows = lax.broadcasted_iota(jnp.int32, (channels, channels), 0)
    lanes = lax.broadcasted_iota(jnp.int32, (channels, channels), 1)
    same = (rows // HD) == (lanes // HD)
    eye = rows == lanes
    head = lax.broadcasted_iota(jnp.int32, (channels, 1), 0) // HD
    sharp = jnp.zeros((channels, 1), F32)
    for h in range(heads):
        sharp = jnp.where(head == h, sharp_ref[h], sharp)

    def to_row(col):
        return jnp.sum(jnp.where(eye, col, 0.0), axis=0, keepdims=True)

    norms = jnp.sqrt(sq + 1e-06) * jnp.sqrt(to_row(sk) + 1e-06)
    logits = jnp.where(same, sharp * gram / norms, 0.0)
    expo = jnp.where(same, jnp.exp(logits), 0.0)
    attend = expo / jnp.sum(expo, axis=1, keepdims=True)
    attend_low = attend.astype(BF16)
    omap_ref[...] = dot_full(mixed, attend_low.astype(F32), NT) / texels
    grad_attend = dot_full(wo_ref[...].astype(F32), mixed, TN)
    grad_logits = attend * (grad_attend - jnp.sum(attend * grad_attend, axis=1, keepdims=True))
    product = grad_logits * logits
    row_terms = jnp.sum(product, axis=1, keepdims=True)
    col_terms = to_col(jnp.sum(product, axis=0, keepdims=True))
    for h in range(heads):
        sharp_adj_ref[h] = jnp.sum(jnp.where(head == h, row_terms, 0.0)) / sharp_ref[h] / texels
    coupling = (sharp * grad_logits / norms).astype(BF16)
    row_scale = row_terms / (sq + 1e-06)
    col_scale = col_terms / (sk + 1e-06)
    cells = conv_ref.shape[1]
    step = 256
    edges = [jnp.zeros((2 * SIDE, channels), F32) for _ in range(3)]
    for n in range(cells // step):
        at = pl.ds(n * step, step)
        queries = conv_ref[pl.ds(0, channels), at]
        keys = conv_ref[pl.ds(channels, channels), at]
        grad_attended = dot(wo_ref[...], g_ref[:, at], TN).astype(BF16)
        grads = (
            dot(coupling, keys) - row_scale * queries.astype(F32),
            dot(coupling, queries, TN) - col_scale * keys.astype(F32),
            dot(attend_low, grad_attended, TN),
        )
        for i, grad in enumerate(grads):
            grad = grad.astype(BF16)
            grad_ref[pl.ds(i * channels, channels), at] = grad
            edges[i] = edges[i] + dot(sel_ref[:, at], grad, NT)
    edge_ref[...] = jnp.concatenate(edges, axis=1).astype(BF16)


def back_kernel(rows, cols, texels, grad_ref, top_ref, bot_ref, side_ref, shift_ref, spread_ref,
                taps_ref, p_ref, normed_ref, wt_ref, x_ref, stat_ref, gain_ref, g_ref,
                out_ref, part_ref, moved, gp_ref, sums):
    width = grad_ref.shape[0]
    channels = width // 3
    part_rows = part_ref.shape[0]
    shift_rows(rows, cols, grad_ref, top_ref, bot_ref, side_ref, shift_ref, spread_ref, moved)

    def chunk(i, carry):
        rs = pl.ds(pl.multiple_of(i * 16, 16), 16)
        taps = [jnp.broadcast_to(taps_ref[rs, pl.ds(k, 1)], (16, 128)) for k in range(9)]
        tap_sums = [jnp.zeros((16, 128), F32) for _ in range(9)]
        for half in range(cols // 128):
            got = {}
            for y in range(rows + 2):
                at = pl.ds(y * cols + half * 128, 128)
                if y == 0:
                    mid = top_ref[rs, pl.ds(half * 128, 128)]
                elif y == rows + 1:
                    mid = bot_ref[rs, pl.ds(half * 128, 128)]
                else:
                    mid = grad_ref[rs, pl.ds((y - 1) * cols + half * 128, 128)]
                got[y] = (moved[0, rs, at].astype(F32), mid.astype(F32), moved[1, rs, at].astype(F32))
                if y >= 2:
                    here = pl.ds((y - 2) * cols + half * 128, 128)
                    field = p_ref[rs, here].astype(F32)
                    out = jnp.zeros((16, 128), F32)
                    for a in range(3):
                        for b in range(3):
                            k = 3 * (2 - a) + (2 - b)
                            out = out + taps[k] * got[y - 2 + a][b]
                            tap_sums[k] = tap_sums[k] + field * got[y - 2 + a][b]
                    gp_ref[rs, here] = out.astype(BF16)
        lane = lax.broadcasted_iota(jnp.int32, (16, 128), 1)
        packed = jnp.zeros((16, 128), F32)
        for k in range(9):
            packed = jnp.where(lane == k, jnp.sum(tap_sums[k], axis=1, keepdims=True), packed)
        sums[rs, :] = packed
        return carry

    lax.fori_loop(0, width // 16, chunk, 0)
    gain = to_col(gain_ref[...])
    gain_sum = jnp.zeros((channels, cols), F32)
    bias_sum = jnp.zeros((channels, cols), F32)
    for y in range(rows):
        at = pl.ds(y * cols, cols)
        grad_normed = dot(wt_ref[...], gp_ref[:, at])
        mean, inv = stat_ref[pl.ds(0, 1), at], stat_ref[pl.ds(1, 1), at]
        x_hat = (x_ref[:, at].astype(F32) - mean) * inv
        gain_sum = gain_sum + grad_normed * x_hat
        bias_sum = bias_sum + grad_normed
        grad_hat = grad_normed * gain
        centre = jnp.sum(grad_hat, axis=0, keepdims=True) / channels
        slope = jnp.sum(grad_hat * x_hat, axis=0, keepdims=True) / channels
        out = g_ref[:, at].astype(F32) + inv * (grad_hat - centre - x_hat * slope)
        out_ref[:, at] = out.astype(BF16)
    lane = lax.broadcasted_iota(jnp.int32, (channels, 128), 1)
    first = sums[pl.ds(0, channels), :]
    first = jnp.where(lane == 9, jnp.sum(gain_sum, axis=1, keepdims=True), first)
    first = jnp.where(lane == 10, jnp.sum(bias_sum, axis=1, keepdims=True), first)
    sums[pl.ds(0, channels), :] = first
    sums[pl.ds(width, 64), :] = jnp.zeros((64, 128), F32)
    weight = dot(normed_ref[...], gp_ref[...], NT) / texels
    whole, half, at = width // 128, channels // 2, 0
    for i in range(whole):
        part_ref[pl.ds(at, channels), :] = weight[:, i * 128:(i + 1) * 128].astype(BF16)
        at += channels
    rest = weight[:, whole * 128:]
    part_ref[pl.ds(at, half), :] = jnp.concatenate([rest[:half], rest[half:]], axis=1).astype(BF16)
    at += half
    for i in range(whole + 1):
        block = jnp.transpose(sums[pl.ds(i * 128, 128), :])[:16]
        part_ref[pl.ds(at, 16), :] = (block / texels).astype(BF16)
        at += 16
    part_ref[pl.ds(at, part_rows - at), :] = jnp.zeros((part_rows - at, 128), BF16)


def call(kernel, out_shape, args, in_specs=None, out_specs=None, scratch=()):
    return pl.pallas_call(
        kernel,
        out_shape=out_shape,
        in_specs=in_specs or [VMEM] * len(args),
        out_specs=out_specs or (VMEM,) * len(out_shape),
        scratch_shapes=scratch,
        compiler_params=pltpu.CompilerParams(vmem_limit_bytes=LIMIT),
    )(*args)


def constants(rows, cols):
    cells, wide = rows * cols, (rows + 2) * cols
    pick = np.zeros((2 * SIDE, cells), np.float32)
    shift = np.zeros((2, cols, cols), np.float32)
    spread = np.zeros((2, 3, SIDE, wide), np.float32)
    for y in range(rows):
        pick[y, y * cols] = 1.0
        pick[SIDE + y, y * cols + cols - 1] = 1.0
    for x in range(cols - 1):
        shift[0, x, x + 1] = 1.0
        shift[1, x + 1, x] = 1.0
    for side, col in ((0, 0), (1, cols - 1)):
        spread[side, 0, rows - 1, col] = 1.0
        for y in range(rows):
            spread[side, 1, y, (y + 1) * cols + col] = 1.0
        spread[side, 2, 0, (rows + 1) * cols + col] = 1.0
    return (
        jnp.asarray(pick, BF16),
        jnp.asarray(shift, BF16),
        jnp.asarray(spread.reshape(2, 3 * SIDE, wide), BF16),
    )


def body(x, g, gain, bias, weight, filter_taps, sharpness, out_matrix):
    channels, rows, cols = x.shape
    cells = rows * cols
    width = weight.shape[0]
    texels = float(cells * lax.axis_size("gy") * lax.axis_size("gx"))
    pick, shift, spread = constants(rows, cols)
    x = x.reshape(channels, cells)
    g = g.reshape(channels, cells)
    gain, bias, weight_t = gain[None, :], bias[None, :], weight.T
    taps = filter_taps.reshape(9, width).T
    shape = jax.ShapeDtypeStruct

    p, normed, stat, edge = call(
        functools.partial(front_kernel, rows, cols),
        (shape((width, cells), BF16), shape((channels, cells), BF16), shape((8, cells), F32),
         shape((2 * SIDE, width), BF16)),
        (x, gain, bias, weight_t, pick),
    )
    top, bot, side = halo(p, edge, cols, 0)
    moved = pltpu.VMEM((2, width, (rows + 2) * cols), BF16)
    conv, part = call(
        functools.partial(conv_kernel, rows, cols),
        (shape((width, cells), BF16), shape((padded_rows(2 * (channels + HD)), 128), F32)),
        (p, top, bot, side, shift, spread, taps, g),
        scratch=(moved, pltpu.VMEM((width, 128), F32)),
    )
    (total,) = sum_over_devices(part, 1, whole_sum, (shape(part.shape, F32),))
    grad, edge, omap_adj, sharp_adj = call(
        functools.partial(attend_kernel, texels),
        (shape((width, cells), BF16), shape((2 * SIDE, width), BF16),
         shape((channels, channels), F32), shape((ATTENDER_TOTAL,), F32)),
        (total, sharpness, out_matrix, conv, g, pick),
        in_specs=[VMEM, SMEM] + [VMEM] * 4,
        out_specs=(VMEM, VMEM, VMEM, SMEM),
    )
    top, bot, side = halo(grad, edge, cols, 2)
    part_rows = width // 128 * channels + channels // 2 + (width // 128 + 1) * 16
    out, part = call(
        functools.partial(back_kernel, rows, cols, texels),
        (shape((channels, cells), BF16), shape((padded_rows(part_rows, 16), 128), BF16)),
        (grad, top, bot, side, shift, spread, taps, p, normed, weight_t, x, stat, gain, g),
        scratch=(moved, pltpu.VMEM((width, cells), BF16), pltpu.VMEM((width + 64, 128), F32)),
    )
    (total,) = sum_over_devices(part, 3, whole_sum, (shape(part.shape, BF16),))
    weight_adj, filter_adj, gain_adj, bias_adj = call(
        parameter_kernel,
        (shape((channels, width), F32), shape((3, 3, width), F32),
         shape((1, channels), F32), shape((1, channels), F32)),
        (total,),
    )
    return (
        out.reshape(channels, rows, cols),
        weight_adj.T,
        filter_adj,
        omap_adj,
        sharp_adj,
        gain_adj.reshape(channels),
        bias_adj.reshape(channels),
    )


def solution(mesh):
    in_specs = (P(None, "gy", "gx"), P(None, "gy", "gx"), P(), P(), P(), P(), P(), P())
    out_specs = (P(None, "gy", "gx"), P(), P(), P(), P(), P(), P())
    return jax.shard_map(body, mesh=mesh, in_specs=in_specs, out_specs=out_specs, check_vma=False)
```
